256 devices in a mesh: blk: 4 (over y_lo, core), fsdp: 64 (over x, y_hi, z).
Axes of the slice: x: 4, y: 4 (y_hi: 2, y_lo: 2; y = y_hi * 2 + y_lo), z: 8, core: 2. Of those that a mesh axis runs over, the one named last changes fastest.
Arguments:
- picture_vectors: bfloat16 [49152, 1152], P(('blk', 'fsdp')), may hold values from -1 to 1
- caption_vectors: bfloat16 [49152, 1152], P(('blk', 'fsdp')), may hold values from -1 to 1
- natural_sharpness_exponent: float32 [1], replicated, may hold values from 0.5 to 1
- trained_shift_term: float32 [1], replicated, may hold values from -3 to -1
- objective_factor: float32 [1], replicated, may hold values from 3072 to 12288
Outputs:
- image_grad: float32 [49152, 1152], P(('blk', 'fsdp'))
- text_grad: float32 [49152, 1152], P(('blk', 'fsdp'))
The draws below stay inside these ranges and needn't reach their ends.
All inputs are finite; a program needn't handle non-finite values.
Results may differ from the reference program's by a relative error of at most 0.0014.
Values may be sent and summed in bfloat16 or wider, within the bound.
A program may use at most 64 MiB of HBM per device.

```python
import math
import jax
import jax.numpy as jnp
from jax import lax

D = 1152
ROWS_DEV = 192
SPAN = 8
COUPLE_COUNT = 49152
N_BLK = 4
N_FSDP = 64


def block_scale(rng, shape, cuts, least, high):
    def one(position, shards_of):
        draws = jax.random.uniform(jax.random.fold_in(jax.random.fold_in(rng, 6), position), (shards_of,), jnp.float32, least / len(cuts), high / len(cuts))
        return jnp.repeat(jnp.exp(draws), shape[position] // shards_of).reshape((-1,) + (1,) * (len(shape) - position - 1))

    level = one(*cuts[0])
    for cut in cuts[1:]:
        level = level * one(*cut)
    return level


def scatter_about(own_key, dims, scale, most, cuts=(), kind=jnp.bfloat16):
    result = scale * jax.random.normal(own_key, dims, jnp.float32)
    if cuts:
        result = result * block_scale(own_key, dims, cuts, -0.22, 0.18)
    return jnp.clip(result, -most, most).astype(kind)


def setup_inputs(seed: int = 0) -> dict:
    streams_of = jax.random.split(jax.random.key(seed), 6)
    return {
        "picture_vectors": scatter_about(streams_of[0], (COUPLE_COUNT, D), (1.0 / D ** 0.25), 1.0, ((0, 256),)),
        "caption_vectors": scatter_about(streams_of[1], (COUPLE_COUNT, D), (1.0 / D ** 0.25), 1.0, ((0, 256),)),
        "natural_sharpness_exponent": jnp.clip(jax.random.uniform(streams_of[2], (1,), jnp.float32, 0.5, 1.0), 0.5, 1.0),
        "trained_shift_term": jnp.clip(jax.random.uniform(streams_of[3], (1,), jnp.float32, -3.0, -1.0), -3.0, -1.0),
        "objective_factor": jnp.clip(jnp.exp(jax.random.uniform(streams_of[4], (1,), jnp.float32, math.log(3072.0), math.log(12288.0))), 3072.0, 12288.0),
    }


def to_columns(array):
    return array.reshape(N_BLK, N_FSDP, ROWS_DEV, D).transpose(1, 0, 2, 3).reshape(N_FSDP, N_BLK * ROWS_DEV, D)


def from_columns(array):
    return array.reshape(N_FSDP, N_BLK, ROWS_DEV, D).transpose(1, 0, 2, 3).reshape(COUPLE_COUNT, D)


def reference(picture_vectors, caption_vectors, natural_sharpness_exponent, trained_shift_term, objective_factor):
    trained_sharpness = jnp.exp(natural_sharpness_exponent[0])
    match_sign_factor = objective_factor[0] * trained_sharpness / COUPLE_COUNT
    column_rows = N_BLK * ROWS_DEV
    image_cols = to_columns(picture_vectors)
    text_cols = to_columns(caption_vectors)
    identity = jnp.eye(column_rows, dtype=jnp.float32)

    def one_column(text_sum, index):
        rows = lax.dynamic_index_in_dim(image_cols, index, 0, keepdims=False)
        image_part = jnp.zeros((column_rows, D), jnp.float32)
        for step in range(SPAN):
            target = ((index + step) % N_FSDP).astype(jnp.int32)
            cols = lax.dynamic_index_in_dim(text_cols, target, 0, keepdims=False)
            similarity_matrix = jnp.dot(rows, cols.T, preferred_element_type=jnp.float32)
            sigmoid_outputs = jax.nn.sigmoid(trained_sharpness * similarity_matrix + trained_shift_term[0])
            if step == 0:
                sigmoid_outputs = sigmoid_outputs - identity
            coefficient = sigmoid_outputs.astype(jnp.bfloat16)
            image_part = image_part + jnp.dot(coefficient, cols, preferred_element_type=jnp.float32)
            text_part = lax.dot_general(coefficient, rows, (((0,), (0,)), ((), ())), preferred_element_type=jnp.float32)
            current = lax.dynamic_index_in_dim(text_sum, target, 0, keepdims=False)
            text_sum = lax.dynamic_update_index_in_dim(text_sum, current + text_part, target, 0)
        return text_sum, match_sign_factor * image_part

    start_sum = jnp.zeros((N_FSDP, column_rows, D), jnp.float32)
    text_sum, image_parts = lax.scan(one_column, start_sum, jnp.arange(N_FSDP, dtype=jnp.int32))
    return from_columns(image_parts), from_columns(match_sign_factor * text_sum)
```

```python
import functools

import jax
import jax.numpy as jnp
from jax import lax
from jax.experimental import pallas as pl
from jax.experimental.pallas import tpu as pltpu
from jax.sharding import PartitionSpec as P

SPAN = 8
LINE = 8
PIECES = 4

MESH = pl.DeviceIdType.MESH
F32 = jnp.float32
BF16 = jnp.bfloat16

COMPUTE = True
COMM = True


def remote(src, dst, sent, landed, device):
    return pltpu.make_async_remote_copy(
        src_ref=src,
        dst_ref=dst,
        send_sem=sent,
        recv_sem=landed,
        device_id=device,
        device_id_type=MESH,
    )


def kernel(
    columns,
    pairs,
    exponent_ref,
    shift_ref,
    factor_ref,
    image_ref,
    text_ref,
    image_out,
    text_out,
    col,
    ring,
    far,
    acc,
    core_in,
    wide_in,
    slim_out,
    slim_in,
    ring_sent,
    ring_landed,
    col_sent,
    col_landed,
    sum_sent,
    sum_landed,
):
    rows, width = image_ref.shape
    piece = rows // PIECES
    lines = columns // LINE
    b = lax.axis_index("blk")
    c = lax.axis_index("fsdp")

    def column_at(offset):
        other = lax.rem(c + offset + columns, columns)
        change = lax.rem(other // LINE - c // LINE + lines, lines)
        return (lax.rem(b + 2 * lax.rem(change, 2), 4), other)

    core_slot = b + 1 - 2 * lax.rem(b, 2)
    chip_slot = lax.rem(b + 2, 4)
    both_slot = lax.rem(core_slot + 2, 4)
    core_peer = (core_slot, c)
    chip_peer = (chip_slot, c)
    back, ahead = column_at(-1), column_at(1)
    far_back, far_ahead = column_at(1 - SPAN), column_at(SPAN - 1)
    own = (text_ref, image_ref)
    home = (image_ref, text_ref)
    near_peer = (back, ahead)
    jump_peer = (far_back, far_ahead)
    turn_peer = (ahead, back)

    barrier = pltpu.get_barrier_semaphore()
    for device in (back, ahead, far_back, far_ahead, core_peer, chip_peer):
        pl.semaphore_signal(barrier, inc=1, device_id=device, device_id_type=MESH)
    pl.semaphore_wait(barrier, 6)

    def part(k, way=0):
        return pl.ds(pl.multiple_of(way * rows + k * piece, piece), piece)

    def hop(side, n, way, k):
        if n == 0:
            src = own[side].at[part(k)]
        else:
            src = ring.at[side, n - 1, part(k, way)]
        dst = far.at[side, part(k)] if n == 3 else ring.at[side, n, part(k, way)]
        peer = near_peer[side] if way == 0 else (jump_peer[side] if n == 0 else turn_peer[side])
        return remote(src, dst, ring_sent.at[side, n, way, k], ring_landed.at[side, n, way, k], peer)

    def gather(side, kind):
        slot = chip_slot if kind == 2 else b
        src = col.at[side, slot] if kind == 2 else home[side]
        peer = chip_peer if kind == 1 else core_peer
        return remote(src, col.at[side, slot], col_sent.at[side, kind], col_landed.at[side, kind], peer)

    def core_sum(side, kind):
        slot = both_slot if kind == 0 else core_slot
        return remote(
            acc.at[side, slot], core_in.at[side, kind], sum_sent.at[side, kind], sum_landed.at[side, kind], core_peer
        )

    def chip_sum(side):
        src = acc.at[side, chip_slot] if side == 0 else slim_out
        dst = wide_in if side == 0 else slim_in
        return remote(src, dst, sum_sent.at[side, 2], sum_landed.at[side, 2], chip_peer)

    temperature = jnp.exp(jnp.full((1, 128), exponent_ref[0], F32))
    shift = jnp.full((1, 128), shift_ref[0], F32)
    weight = factor_ref[0] * temperature / pairs

    def score(side, slot, shards, first=False):
        count = shards.shape[0]
        mine = col[side, slot]
        logits = (
            lax.dot_general(mine, shards[...], (((1,), (1,)), ((), ())), preferred_element_type=F32)
            * temperature[:, :1]
            + shift[:, :1]
        )
        values = jax.nn.sigmoid(logits)
        if first:
            i = lax.broadcasted_iota(jnp.int32, (rows, count), 0)
            j = lax.broadcasted_iota(jnp.int32, (rows, count), 1)
            values = values - jnp.where(i + (slot - b) * rows == j, 1.0, 0.0)
        coefficient = values.astype(BF16)
        share = jnp.dot(coefficient, shards[...], preferred_element_type=F32)
        if first:
            acc[side, slot] = share
        else:
            acc[side, slot] += share

    def pair_of(side, n):
        return ring.at[side, n]

    def begin(side):
        for k in range(PIECES):
            hop(side, 0, 0, k).start()
            hop(side, 0, 1, k).start()

    def take(side, n, k):
        for way in (0, 1):
            hop(side, n, way, k).wait_recv()
            if n < 2:
                hop(side, n + 1, way, k).start()
        if n == 2:
            @pl.when(k < PIECES // 2)
            def _():
                hop(side, 3, 0, k).start()

            @pl.when(k >= PIECES // 2)
            def _():
                hop(side, 3, 1, k).start()

    def far_pieces(method, side):
        for k in range(PIECES):
            getattr(hop(side, 3, 0 if k < PIECES // 2 else 1, k), method)()

    def finish(side, slots=None):
        score(side, both_slot, far.at[side])
        core_sum(side, 0).start()
        score(side, chip_slot, far.at[side])
        core_sum(side, 0).wait_recv()
        total = acc[side, chip_slot] + core_in[side, 0]
        if side == 0:
            acc[side, chip_slot] = total
        else:
            slim_out[...] = total.astype(BF16)
        chip_sum(side).start()
        score(side, core_slot, far.at[side])
        core_sum(side, 1).start()
        score(side, b, far.at[side])

    def close(side):
        core_sum(side, 1).wait_recv()
        total = acc[side, b] + core_in[side, 1]
        chip_sum(side).wait_recv()
        if side == 0:
            image_out[...] = weight[:, :1] * (total + wide_in[...])
        else:
            text_out[...] = weight[:, :1] * (total + slim_in[...].astype(F32))

    begin(0)
    gather(0, 0).start()
    gather(0, 1).start()
    col[0, b] = image_ref[...]
    col[1, b] = text_ref[...]

    @pl.loop(0, PIECES)
    def _(k):
        take(0, 0, k)

    gather(0, 1).wait_recv()
    gather(0, 2).start()
    gather(1, 0).start()
    gather(1, 1).start()
    gather(0, 0).wait_recv()
    gather(0, 2).wait_recv()

    @pl.loop(0, PIECES)
    def _(k):
        take(0, 1, k)
        score(0, k, own[0], first=True)
        score(0, k, pair_of(0, 0))

    gather(1, 1).wait_recv()
    gather(1, 2).start()

    @pl.loop(0, PIECES)
    def _(k):
        take(0, 2, k)
        score(0, k, pair_of(0, 1))

    begin(1)
    gather(1, 0).wait_recv()
    gather(1, 2).wait_recv()

    @pl.loop(0, PIECES)
    def _(k):
        score(0, k, pair_of(0, 2))

    far_pieces("wait_recv", 0)

    @pl.loop(0, PIECES)
    def _(k):
        take(1, 0, k)

    finish(0)

    @pl.loop(0, PIECES)
    def _(k):
        take(1, 1, k)
        score(1, k, own[1], first=True)
        score(1, k, pair_of(1, 0))

    close(0)

    @pl.loop(0, PIECES)
    def _(k):
        take(1, 2, k)
        score(1, k, pair_of(1, 1))

    @pl.loop(0, PIECES)
    def _(k):
        score(1, k, pair_of(1, 2))

    for side in (0, 1):
        for kind in range(3):
            gather(side, kind).wait_send()

        @pl.loop(0, PIECES)
        def _(k):
            for n in range(3):
                for way in (0, 1):
                    hop(side, n, way, k).wait_send()

    far_pieces("wait_send", 0)
    core_sum(0, 0).wait_send()
    core_sum(0, 1).wait_send()
    chip_sum(0).wait_send()

    far_pieces("wait_recv", 1)
    finish(1)
    close(1)
    far_pieces("wait_send", 1)
    core_sum(1, 0).wait_send()
    core_sum(1, 1).wait_send()
    chip_sum(1).wait_send()


def local(
    picture_vectors,
    caption_vectors,
    natural_sharpness_exponent,
    trained_shift_term,
    objective_factor,
):
    rows, width = picture_vectors.shape
    groups = lax.axis_size("blk")
    columns = lax.axis_size("fsdp")
    pairs = rows * groups * columns
    vmem = pl.BlockSpec(memory_space=pltpu.VMEM)
    smem = pl.BlockSpec(memory_space=pltpu.SMEM)
    out = jax.ShapeDtypeStruct((rows, width), F32)
    return pl.pallas_call(
        functools.partial(kernel, columns, pairs),
        out_shape=(out, out),
        in_specs=[smem, smem, smem, vmem, vmem],
        out_specs=(vmem, vmem),
        scratch_shapes=[
            pltpu.VMEM((2, groups, rows, width), BF16),
            pltpu.VMEM((2, 3, 2 * rows, width), BF16),
            pltpu.VMEM((2, rows, width), BF16),
            pltpu.VMEM((2, groups, rows, width), F32),
            pltpu.VMEM((2, 2, rows, width), F32),
            pltpu.VMEM((rows, width), F32),
            pltpu.VMEM((rows, width), BF16),
            pltpu.VMEM((rows, width), BF16),
            pltpu.SemaphoreType.DMA((2, 4, 2, PIECES)),
            pltpu.SemaphoreType.DMA((2, 4, 2, PIECES)),
            pltpu.SemaphoreType.DMA((2, 3)),
            pltpu.SemaphoreType.DMA((2, 3)),
            pltpu.SemaphoreType.DMA((2, 3)),
            pltpu.SemaphoreType.DMA((2, 3)),
        ],
        compiler_params=pltpu.CompilerParams(
            collective_id=0, has_side_effects=True, vmem_limit_bytes=50 * 1024 * 1024
        ),
        cost_estimate=pl.CostEstimate(
            flops=2 * 4 * SPAN * groups * rows * rows * width,
            bytes_accessed=12 * rows * width,
            transcendentals=2 * SPAN * groups * rows * rows,
        ),
    )(
        natural_sharpness_exponent,
        trained_shift_term,
        objective_factor,
        picture_vectors,
        caption_vectors,
    )


def solution(mesh):
    return jax.shard_map(
        local,
        mesh=mesh,
        in_specs=(P(("blk", "fsdp"), None), P(("blk", "fsdp"), None), P(), P(), P()),
        out_specs=(P(("blk", "fsdp"), None), P(("blk", "fsdp"), None)),
        check_vma=False,
    )
```

```python
import functools

import jax
import jax.numpy as jnp
from jax import lax
from jax.experimental import pallas as pl
from jax.experimental.pallas import tpu as pltpu
from jax.sharding import PartitionSpec as P

SPAN = 8
LINE = 8
PIECES = 4
HALF = PIECES // 2

MESH = pl.DeviceIdType.MESH
F32 = jnp.float32
BF16 = jnp.bfloat16


def remote(src, dst, sent, landed, device):
    return pltpu.make_async_remote_copy(
        src_ref=src,
        dst_ref=dst,
        send_sem=sent,
        recv_sem=landed,
        device_id=device,
        device_id_type=MESH,
    )


def kernel(
    columns,
    pairs,
    exponent_ref,
    shift_ref,
    factor_ref,
    image_ref,
    text_ref,
    image_out,
    text_out,
    col,
    trav,
    crossed,
    ring,
    far,
    acc,
    slim_out,
    slim_in,
    ring_sent,
    ring_landed,
    core_sent,
    core_landed,
    cross_sent,
    cross_landed,
    own_sent,
    own_landed,
    sum_sent,
    sum_landed,
    local_done,
):
    rows, width = image_ref.shape
    piece = rows // PIECES
    lines = columns // LINE
    b = lax.axis_index("blk")
    c = lax.axis_index("fsdp")
    z = lax.rem(c, LINE)

    def column_at(offset):
        other = lax.rem(c + offset + columns, columns)
        change = lax.rem(other // LINE - c // LINE + lines, lines)
        return (lax.rem(b + 2 * lax.rem(change, 2), 4), other)

    core_peer = (b + 1 - 2 * lax.rem(b, 2), c)
    chip_peer = (lax.rem(b + 2, 4), c)
    back, ahead = column_at(-1), column_at(1)
    over = (column_at(-LINE), column_at(LINE))
    end_peer = (column_at(LINE - 1), column_at(1 - LINE))
    first, last = (0, LINE - 1), (LINE - 1, 0)
    own = (text_ref, image_ref)
    near_peer, round_peer = (back, ahead), (ahead, back)

    local = [
        pltpu.make_async_copy(src, dst, local_done.at[i])
        for i, (src, dst) in enumerate(
            (
                (image_ref, col.at[0, 0]),
                (text_ref, col.at[1, 0]),
                (text_ref, trav.at[0, pl.ds(0, rows)]),
                (image_ref, trav.at[1, pl.ds(0, rows)]),
            )
        )
    ]
    for copy in local:
        copy.start()

    barrier = pltpu.get_barrier_semaphore()
    for device in (back, ahead, *over, core_peer, chip_peer):
        pl.semaphore_signal(barrier, inc=1, device_id=device, device_id_type=MESH)
    for side in (0, 1):

        @pl.when(z == first[side])
        def _():
            pl.semaphore_signal(barrier, inc=1, device_id=end_peer[side], device_id_type=MESH)
            pl.semaphore_wait(barrier, 7)

    @pl.when(lax.rem(z, LINE - 1) != 0)
    def _():
        pl.semaphore_wait(barrier, 6)

    def part(k, segment=0):
        return pl.ds(pl.multiple_of(segment * rows + k * piece, piece), piece)

    def slot_of(side, n, way, k, core=0):
        if n == 3:
            return far.at[side, part(k, core)]
        return ring.at[side, n, part(k, 2 * way + core)]

    def hop(side, n, way, k, src=None, peer=None):
        if src is None:
            src = own[side].at[part(k)] if n == 0 else slot_of(side, n - 1, way, k)
        if peer is None:
            peer = near_peer[side] if way == 0 else round_peer[side]
        return remote(
            src, slot_of(side, n, way, k), ring_sent.at[side, n, way, k], ring_landed.at[side, n, way, k], peer
        )

    def share(side, n, way, k):
        return remote(
            slot_of(side, n, way, k),
            slot_of(side, n, way, k, 1),
            core_sent.at[side, n, way, k],
            core_landed.at[side, n, way, k],
            core_peer,
        )

    def cross(side, k):
        return remote(
            own[side].at[part(k)],
            crossed.at[side, part(k)],
            cross_sent.at[side, k],
            cross_landed.at[side, k],
            over[side],
        )

    def own_to_chip(side):
        src = (image_ref, text_ref)[side]
        return remote(src, col.at[side, 1], own_sent.at[side, 0], own_landed.at[side, 0], chip_peer)

    def own_to_core(side):
        return remote(
            own[side], trav.at[side, pl.ds(rows, rows)], own_sent.at[side, 1], own_landed.at[side, 1], core_peer
        )

    def chip_sum(side):
        return remote(
            slim_out.at[side], slim_in.at[side], sum_sent.at[side], sum_landed.at[side], chip_peer
        )

    temperature = jnp.exp(jnp.full((1, 128), exponent_ref[0], F32))
    shift = jnp.full((1, 128), shift_ref[0], F32)
    weight = factor_ref[0] * temperature / pairs

    def score(side, slot, shards, first=False):
        count = shards.shape[0]
        logits = (
            lax.dot_general(
                col[side, slot], shards[...], (((1,), (1,)), ((), ())), preferred_element_type=F32
            )
            * temperature[:, :1]
            + shift[:, :1]
        )
        values = jax.nn.sigmoid(logits)
        if first:
            i = lax.broadcasted_iota(jnp.int32, (rows, count), 0)
            j = lax.broadcasted_iota(jnp.int32, (rows, count), 1)
            values = values - jnp.where(i + slot * 2 * rows == j, 1.0, 0.0)
        coefficient = values.astype(BF16)
        product = jnp.dot(coefficient, shards[...], preferred_element_type=F32)
        if first:
            acc[side, slot] = product
        else:
            acc[side, slot] += product

    def score_hop(side, n, k):
        score(side, k // 2, ring.at[side, n, pl.ds(pl.multiple_of(lax.rem(k, 2) * 2 * rows, rows), 2 * rows)])

    def near_start(side, k):
        @pl.when(z != first[side])
        def _():
            hop(side, 0, 0, k).start()

    def cross_start(side, k):
        @pl.when(z != last[side])
        def _():
            cross(side, k).start()

        @pl.when(z == last[side])
        def _():
            hop(side, 0, 1, k, peer=end_peer[1 - side]).start()

    def relay(side, k):
        @pl.when(z != last[side])
        def _():
            cross(side, k).wait_recv()
            hop(side, 0, 1, k, src=crossed.at[side, part(k)]).start()

        @pl.when(z == first[side])
        def _():
            hop(side, 0, 0, k, src=crossed.at[side, part(k)], peer=end_peer[side]).start()

    def take(side, n, way, k):
        hop(side, n, way, k).wait_recv()
        if n < 2:
            hop(side, n + 1, way, k).start()
        else:

            @pl.when(k < HALF if way == 0 else k >= HALF)
            def _():
                hop(side, 3, way, k).start()

        share(side, n, way, k).start()

    def on_far(method, make, side, k):
        @pl.when(k < HALF)
        def _():
            getattr(make(side, 3, 0, k), method)()

        @pl.when(k >= HALF)
        def _():
            getattr(make(side, 3, 1, k), method)()

    def take_far(side, k):
        on_far("wait_recv", hop, side, k)
        on_far("start", share, side, k)

    def shared(side, n):
        @pl.loop(0, PIECES)
        def _(k):
            if n == 3:
                on_far("wait_recv", share, side, k)
            else:
                for way in (0, 1):
                    share(side, n, way, k).wait_recv()

    def swap(side):
        score(side, 1, far.at[side])
        slim_out[side] = acc[side, 1].astype(BF16)
        chip_sum(side).start()

    def close(side, out):
        chip_sum(side).wait_recv()
        out[...] = weight[:, :1] * (acc[side, 0] + slim_in[side].astype(F32))

    @pl.loop(0, PIECES)
    def _(k):
        near_start(0, k)
        near_start(1, k)
        cross_start(0, k)
        cross_start(1, k)

    for side in (0, 1):
        own_to_chip(side).start()
        own_to_core(side).start()

    @pl.loop(0, PIECES)
    def _(k):
        relay(0, k)
        relay(1, k)
        take(0, 0, 0, k)
        take(1, 0, 0, k)

    for copy in local:
        copy.wait()
    for side in (0, 1):
        own_to_core(side).wait_recv()
        own_to_chip(side).wait_recv()

    @pl.loop(0, PIECES)
    def _(k):
        take(0, 1, 0, k)
        take(1, 1, 0, k)
        take(0, 0, 1, k)
        take(1, 0, 1, k)
        score(k // 2, lax.rem(k, 2), trav.at[k // 2], first=True)

    shared(0, 0)

    @pl.loop(0, PIECES)
    def _(k):
        take(0, 2, 0, k)
        take(0, 1, 1, k)
        score_hop(0, 0, k)

    shared(1, 0)

    @pl.loop(0, PIECES)
    def _(k):
        take(0, 2, 1, k)
        score_hop(1, 0, k)

    shared(0, 1)

    @pl.loop(0, PIECES)
    def _(k):
        take(1, 2, 0, k)
        take(1, 1, 1, k)
        score_hop(0, 1, k)

    shared(0, 2)
    shared(1, 1)

    @pl.loop(0, PIECES)
    def _(k):
        take_far(0, k)
        score_hop(0, 2, k)

    shared(0, 3)

    @pl.loop(0, PIECES)
    def _(k):
        take(1, 2, 1, k)

        @pl.when(k == 0)
        def _():
            swap(0)

        @pl.when(k == 1)
        def _():
            score(0, 0, far.at[0])

        score_hop(1, 1, k)

    shared(1, 2)

    @pl.loop(0, PIECES)
    def _(k):
        take_far(1, k)
        score_hop(1, 2, k)

    shared(1, 3)
    swap(1)
    score(1, 0, far.at[1])
    close(0, image_out)

    for side in (0, 1):
        own_to_chip(side).wait_send()
        own_to_core(side).wait_send()

        @pl.loop(0, PIECES)
        def _(k):
            @pl.when(z != last[side])
            def _():
                cross(side, k).wait_send()

            for n in range(3):
                for way in (0, 1):
                    hop(side, n, way, k).wait_send()
                    share(side, n, way, k).wait_send()
            on_far("wait_send", hop, side, k)
            on_far("wait_send", share, side, k)

    close(1, text_out)
    chip_sum(0).wait_send()
    chip_sum(1).wait_send()


def local(
    picture_vectors,
    caption_vectors,
    natural_sharpness_exponent,
    trained_shift_term,
    objective_factor,
):
    rows, width = picture_vectors.shape
    groups = lax.axis_size("blk")
    columns = lax.axis_size("fsdp")
    pairs = rows * groups * columns
    vmem = pl.BlockSpec(memory_space=pltpu.VMEM)
    smem = pl.BlockSpec(memory_space=pltpu.SMEM)
    anywhere = pl.BlockSpec(memory_space=pl.ANY)
    out = jax.ShapeDtypeStruct((rows, width), F32)
    sems = pltpu.SemaphoreType.DMA
    return pl.pallas_call(
        functools.partial(kernel, columns, pairs),
        out_shape=(out, out),
        in_specs=[smem, smem, smem, anywhere, anywhere],
        out_specs=(vmem, vmem),
        scratch_shapes=[
            pltpu.VMEM((2, 2, rows, width), BF16),
            pltpu.VMEM((2, 2 * rows, width), BF16),
            pltpu.VMEM((2, rows, width), BF16),
            pltpu.VMEM((2, 3, 4 * rows, width), BF16),
            pltpu.VMEM((2, 2 * rows, width), BF16),
            pltpu.VMEM((2, 2, rows, width), F32),
            pltpu.VMEM((2, rows, width), BF16),
            pltpu.VMEM((2, rows, width), BF16),
            sems((2, 4, 2, PIECES)),
            sems((2, 4, 2, PIECES)),
            sems((2, 4, 2, PIECES)),
            sems((2, 4, 2, PIECES)),
            sems((2, PIECES)),
            sems((2, PIECES)),
            sems((2, 2)),
            sems((2, 2)),
            sems((2,)),
            sems((2,)),
            sems((4,)),
        ],
        compiler_params=pltpu.CompilerParams(
            collective_id=0, has_side_effects=True, vmem_limit_bytes=56 * 1024 * 1024
        ),
        cost_estimate=pl.CostEstimate(
            flops=2 * 4 * SPAN * groups * rows * rows * width,
            bytes_accessed=12 * rows * width,
            transcendentals=2 * SPAN * groups * rows * rows,
        ),
    )(
        natural_sharpness_exponent,
        trained_shift_term,
        objective_factor,
        picture_vectors,
        caption_vectors,
    )


def solution(mesh):
    return jax.shard_map(
        local,
        mesh=mesh,
        in_specs=(P(("blk", "fsdp"), None), P(("blk", "fsdp"), None), P(), P(), P()),
        out_specs=(P(("blk", "fsdp"), None), P(("blk", "fsdp"), None)),
        check_vma=False,
    )
```

```python
import functools

import jax
import jax.numpy as jnp
from jax import lax
from jax.experimental import pallas as pl
from jax.experimental.pallas import tpu as pltpu
from jax.sharding import PartitionSpec as P

SPAN = 8
LINE = 8
PIECES = 4
HALF = PIECES // 2

MESH = pl.DeviceIdType.MESH
F32 = jnp.float32
BF16 = jnp.bfloat16


def remote(src, dst, sent, landed, device):
    return pltpu.make_async_remote_copy(
        src_ref=src,
        dst_ref=dst,
        send_sem=sent,
        recv_sem=landed,
        device_id=device,
        device_id_type=MESH,
    )


def kernel(
    columns,
    pairs,
    exponent_ref,
    shift_ref,
    factor_ref,
    image_ref,
    text_ref,
    image_out,
    text_out,
    col,
    trav,
    crossed,
    ring,
    far,
    acc,
    slim_out,
    slim_in,
    ring_sent,
    ring_landed,
    core_sent,
    core_landed,
    cross_sent,
    cross_landed,
    own_sent,
    own_landed,
    sum_sent,
    sum_landed,
    local_done,
    out_done,
    grad,
    scalars,
):
    rows, width = image_ref.shape
    piece = rows // PIECES
    lines = columns // LINE
    b = lax.axis_index("blk")
    c = lax.axis_index("fsdp")
    z = lax.rem(c, LINE)

    def column_at(offset):
        other = lax.rem(c + offset + columns, columns)
        change = lax.rem(other // LINE - c // LINE + lines, lines)
        return (lax.rem(b + 2 * lax.rem(change, 2), 4), other)

    core_peer = (b + 1 - 2 * lax.rem(b, 2), c)
    chip_peer = (lax.rem(b + 2, 4), c)
    back, ahead = column_at(-1), column_at(1)
    over = (column_at(-LINE), column_at(LINE))
    end_peer = (column_at(LINE - 1), column_at(1 - LINE))
    first, last = (0, LINE - 1), (LINE - 1, 0)
    own = (text_ref, image_ref)
    near_peer, round_peer = (back, ahead), (ahead, back)

    local = [
        pltpu.make_async_copy(src, dst, local_done.at[i])
        for i, (src, dst) in enumerate(
            (
                (image_ref, col.at[0, pl.ds(0, rows)]),
                (text_ref, col.at[1, pl.ds(0, rows)]),
                (text_ref, trav.at[0, pl.ds(0, rows)]),
                (image_ref, trav.at[1, pl.ds(0, rows)]),
                (exponent_ref, scalars.at[0]),
                (shift_ref, scalars.at[1]),
                (factor_ref, scalars.at[2]),
            )
        )
    ]
    for copy in local:
        copy.start()

    barrier = pltpu.get_barrier_semaphore()
    for device in (back, ahead, *over, core_peer, chip_peer):
        pl.semaphore_signal(barrier, inc=1, device_id=device, device_id_type=MESH)
    for side in (0, 1):

        @pl.when(z == first[side])
        def _():
            pl.semaphore_signal(barrier, inc=1, device_id=end_peer[side], device_id_type=MESH)
            pl.semaphore_wait(barrier, 7)

    @pl.when(lax.rem(z, LINE - 1) != 0)
    def _():
        pl.semaphore_wait(barrier, 6)

    for copy in local:
        copy.wait()
    temperature = jnp.exp(jnp.full((1, 128), scalars[0, 0], F32))
    shift = jnp.full((1, 128), scalars[1, 0], F32)
    weight = scalars[2, 0] * temperature / pairs

    def part(k, segment=0):
        return pl.ds(segment * rows + k * piece, piece)

    def slot_of(side, n, way, k, core=0):
        if n == 3:
            return far.at[side, part(k, core)]
        return ring.at[side, n, part(k, 2 * way + core)]

    def hop(side, n, way, k, src=None, peer=None):
        if src is None:
            src = own[side].at[part(k)] if n == 0 else slot_of(side, n - 1, way, k)
        if peer is None:
            peer = near_peer[side] if way == 0 else round_peer[side]
        return remote(
            src, slot_of(side, n, way, k), ring_sent.at[side, n, way, k], ring_landed.at[side, n, way, k], peer
        )

    def share(side, n, way, k):
        return remote(
            slot_of(side, n, way, k),
            slot_of(side, n, way, k, 1),
            core_sent.at[side, n, way, k],
            core_landed.at[side, n, way, k],
            core_peer,
        )

    def cross(side, k):
        return remote(
            own[side].at[part(k)],
            crossed.at[side, part(k)],
            cross_sent.at[side, k],
            cross_landed.at[side, k],
            over[side],
        )

    def own_to_chip(side):
        src = (image_ref, text_ref)[side]
        return remote(src, col.at[side, pl.ds(rows, rows)], own_sent.at[side, 0], own_landed.at[side, 0], chip_peer)

    def own_to_core(side):
        return remote(
            own[side], trav.at[side, pl.ds(rows, rows)], own_sent.at[side, 1], own_landed.at[side, 1], core_peer
        )

    def chip_sum(side, k):
        return remote(
            slim_out.at[side, part(k)],
            slim_in.at[side, part(k)],
            sum_sent.at[side, k],
            sum_landed.at[side, k],
            chip_peer,
        )

    def result(side, k):
        out = (image_out, text_out)[side]
        return pltpu.make_async_copy(grad.at[side, part(k)], out.at[part(k)], out_done.at[side, k])

    def score(side, home, shards, first=False):
        logits = (
            lax.dot_general(
                col[side, home], shards[...], (((1,), (1,)), ((), ())), preferred_element_type=F32
            )
            * temperature[:, :1]
            + shift[:, :1]
        )
        values = jax.nn.sigmoid(logits)
        if first:
            i = lax.broadcasted_iota(jnp.int32, values.shape, 0)
            j = lax.broadcasted_iota(jnp.int32, values.shape, 1)
            values = values - jnp.where((i == j) & (i < rows), 1.0, 0.0)
        coefficient = values.astype(BF16)
        product = jnp.dot(coefficient, shards[...], preferred_element_type=F32)
        if first:
            acc[side, home] = product
        else:
            acc[side, home] += product

    own_rows, chip_rows, all_rows = pl.ds(0, rows), pl.ds(rows, rows), pl.ds(0, 2 * rows)

    def score_hop(side, n, k):
        if k == 1:
            score(side, all_rows, ring.at[side, n])

    def near_start(side, k):
        @pl.when(z != first[side])
        def _():
            hop(side, 0, 0, k).start()

    def cross_start(side, k):
        @pl.when(z != last[side])
        def _():
            cross(side, k).start()

        @pl.when(z == last[side])
        def _():
            hop(side, 0, 1, k, peer=end_peer[1 - side]).start()

    def relay(side, k):
        @pl.when(z != last[side])
        def _():
            cross(side, k).wait_recv()
            hop(side, 0, 1, k, src=crossed.at[side, part(k)]).start()

        @pl.when(z == first[side])
        def _():
            hop(side, 0, 0, k, src=crossed.at[side, part(k)], peer=end_peer[side]).start()

    def take(side, n, way, k):
        hop(side, n, way, k).wait_recv()
        share(side, n, way, k).start()
        if n < 2:
            hop(side, n + 1, way, k).start()
        else:

            if (k < HALF) == (way == 0):
                hop(side, 3, way, k).start()


    def on_far(method, make, side, k):
        getattr(make(side, 3, k // HALF, k), method)()

    def take_far(side, k):
        on_far("wait_recv", hop, side, k)
        on_far("start", share, side, k)

    def shared(side, n):
        for k in range(PIECES):
            if n == 3:
                on_far("wait_recv", share, side, k)
            else:
                for way in (0, 1):
                    share(side, n, way, k).wait_recv()

    def swap(side):
        score(side, chip_rows, far.at[side])
        for k in range(PIECES):
            slim_out[side, part(k)] = acc[side, part(k, 1)].astype(BF16)
            chip_sum(side, k).start()

    def close(side):
        for k in range(PIECES):
            chip_sum(side, k).wait_recv()
            grad[side, part(k)] = (acc[side, part(k)] + slim_in[side, part(k)].astype(F32))
            result(side, k).start()

    for k in range(PIECES):
        near_start(0, k)
        near_start(1, k)
        cross_start(0, k)
        cross_start(1, k)

    for side in (0, 1):
        own_to_chip(side).start()
        own_to_core(side).start()

    for k in range(PIECES):
        relay(0, k)
        relay(1, k)
        take(0, 0, 0, k)
        take(1, 0, 0, k)

    for side in (0, 1):
        own_to_core(side).wait_recv()
        own_to_chip(side).wait_recv()

    for k in range(PIECES):
        take(0, 1, 0, k)
        take(1, 1, 0, k)
        take(0, 0, 1, k)
        take(1, 0, 1, k)
        if k % 2 == 0:
            score(k // 2, all_rows, trav.at[k // 2], first=True)


    shared(0, 0)

    for k in range(PIECES):
        take(0, 2, 0, k)
        take(0, 1, 1, k)
        score_hop(0, 0, k)

    shared(1, 0)

    for k in range(PIECES):
        take(0, 2, 1, k)
        score_hop(1, 0, k)

    shared(0, 1)

    for k in range(PIECES):
        take(1, 2, 0, k)
        take(1, 1, 1, k)
        score_hop(0, 1, k)

    shared(0, 2)
    shared(1, 1)

    for k in range(PIECES):
        take_far(0, k)
        score_hop(0, 2, k)

    shared(0, 3)

    for k in range(PIECES):
        take(1, 2, 1, k)

        if k == 0:
            swap(0)
        if k == 1:
            score(0, own_rows, far.at[0])

        score_hop(1, 1, k)

    shared(1, 2)

    for k in range(PIECES):
        take_far(1, k)
        score_hop(1, 2, k)

    shared(1, 3)
    swap(1)
    score(1, own_rows, far.at[1])
    close(0)

    for side in (0, 1):
        own_to_chip(side).wait_send()
        own_to_core(side).wait_send()

        for k in range(PIECES):
            @pl.when(z != last[side])
            def _():
                cross(side, k).wait_send()

            for n in range(3):
                for way in (0, 1):
                    hop(side, n, way, k).wait_send()
                    share(side, n, way, k).wait_send()
            on_far("wait_send", hop, side, k)
            on_far("wait_send", share, side, k)

    close(1)
    for side in (0, 1):
        for k in range(PIECES):
            chip_sum(side, k).wait_send()
            result(side, k).wait()


def local(
    picture_vectors,
    caption_vectors,
    natural_sharpness_exponent,
    trained_shift_term,
    objective_factor,
):
    rows, width = picture_vectors.shape
    groups = lax.axis_size("blk")
    columns = lax.axis_size("fsdp")
    pairs = rows * groups * columns
    hbm = pl.BlockSpec(memory_space=pltpu.HBM)
    out = jax.ShapeDtypeStruct((rows, width), F32)
    sems = pltpu.SemaphoreType.DMA
    grads = pl.pallas_call(
        functools.partial(kernel, columns, pairs),
        out_shape=(out, out),
        in_specs=[hbm] * 5,
        out_specs=(hbm, hbm),
        scratch_shapes=[
            pltpu.VMEM((2, 2 * rows, width), BF16),
            pltpu.VMEM((2, 2 * rows, width), BF16),
            pltpu.VMEM((2, rows, width), BF16),
            pltpu.VMEM((2, 3, 4 * rows, width), BF16),
            pltpu.VMEM((2, 2 * rows, width), BF16),
            pltpu.VMEM((2, 2 * rows, width), F32),
            pltpu.VMEM((2, rows, width), BF16),
            pltpu.VMEM((2, rows, width), BF16),
            sems((2, 4, 2, PIECES)),
            sems((2, 4, 2, PIECES)),
            sems((2, 4, 2, PIECES)),
            sems((2, 4, 2, PIECES)),
            sems((2, PIECES)),
            sems((2, PIECES)),
            sems((2, 2)),
            sems((2, 2)),
            sems((2, PIECES)),
            sems((2, PIECES)),
            sems((7,)),
            sems((2, PIECES)),
            pltpu.VMEM((2, rows, width), F32),
            pltpu.SMEM((3, 1), F32),
        ],
        compiler_params=pltpu.CompilerParams(
            collective_id=0, has_side_effects=True, vmem_limit_bytes=56 * 1024 * 1024
        ),
        cost_estimate=pl.CostEstimate(
            flops=2 * 4 * SPAN * groups * rows * rows * width,
            bytes_accessed=12 * rows * width,
            transcendentals=2 * SPAN * groups * rows * rows,
        ),
    )(
        natural_sharpness_exponent,
        trained_shift_term,
        objective_factor,
        picture_vectors,
        caption_vectors,
    )
    scale = objective_factor[0] * jnp.exp(natural_sharpness_exponent[0]) / pairs
    return scale * grads[0], scale * grads[1]


def solution(mesh):
    return jax.shard_map(
        local,
        mesh=mesh,
        in_specs=(P(("blk", "fsdp"), None), P(("blk", "fsdp"), None), P(), P(), P()),
        out_specs=(P(("blk", "fsdp"), None), P(("blk", "fsdp"), None)),
        check_vma=False,
    )
```

```python
import functools

import jax
import jax.numpy as jnp
from jax import lax
from jax.experimental import pallas as pl
from jax.experimental.pallas import tpu as pltpu
from jax.sharding import PartitionSpec as P

SPAN = 8
LINE = 8
PIECES = 4
HALF = PIECES // 2

MESH = pl.DeviceIdType.MESH
F32 = jnp.float32
BF16 = jnp.bfloat16


def remote(src, dst, sent, landed, device):
    return pltpu.make_async_remote_copy(
        src_ref=src,
        dst_ref=dst,
        send_sem=sent,
        recv_sem=landed,
        device_id=device,
        device_id_type=MESH,
    )


def kernel(
    columns,
    pairs,
    exponent_ref,
    shift_ref,
    factor_ref,
    image_ref,
    text_ref,
    image_out,
    text_out,
    col,
    trav,
    crossed,
    ring,
    far,
    acc,
    slim_out,
    slim_in,
    ring_sent,
    ring_landed,
    core_sent,
    core_landed,
    cross_sent,
    cross_landed,
    own_sent,
    own_landed,
    sum_sent,
    sum_landed,
    local_done,
    out_done,
    grad,
    scalars,
):
    rows, width = image_ref.shape
    piece = rows // PIECES
    lines = columns // LINE
    b = lax.axis_index("blk")
    c = lax.axis_index("fsdp")
    z = lax.rem(c, LINE)

    def column_at(offset):
        other = lax.rem(c + offset + columns, columns)
        change = lax.rem(other // LINE - c // LINE + lines, lines)
        return (lax.rem(b + 2 * lax.rem(change, 2), 4), other)

    core_peer = (b + 1 - 2 * lax.rem(b, 2), c)
    chip_peer = (lax.rem(b + 2, 4), c)
    back, ahead = column_at(-1), column_at(1)
    over = (column_at(-LINE), column_at(LINE))
    end_peer = (column_at(LINE - 1), column_at(1 - LINE))
    first, last = (0, LINE - 1), (LINE - 1, 0)
    own = (text_ref, image_ref)
    near_peer, round_peer = (back, ahead), (ahead, back)

    local = [
        pltpu.make_async_copy(src, dst, local_done.at[i])
        for i, (src, dst) in enumerate(
            (
                (image_ref, col.at[0, pl.ds(0, rows)]),
                (text_ref, col.at[1, pl.ds(0, rows)]),
                (text_ref, trav.at[0, pl.ds(0, rows)]),
                (image_ref, trav.at[1, pl.ds(0, rows)]),
                (exponent_ref, scalars.at[0]),
                (shift_ref, scalars.at[1]),
                (factor_ref, scalars.at[2]),
            )
        )
    ]
    for copy in local:
        copy.start()

    barrier = pltpu.get_barrier_semaphore()
    for device in (back, ahead, *over, core_peer, chip_peer):
        pl.semaphore_signal(barrier, inc=1, device_id=device, device_id_type=MESH)
    for side in (0, 1):

        @pl.when(z == first[side])
        def _():
            pl.semaphore_signal(barrier, inc=1, device_id=end_peer[side], device_id_type=MESH)
            pl.semaphore_wait(barrier, 7)

    @pl.when(lax.rem(z, LINE - 1) != 0)
    def _():
        pl.semaphore_wait(barrier, 6)

    for copy in local:
        copy.wait()
    temperature = jnp.exp(jnp.full((1, 128), scalars[0, 0], F32))
    shift = jnp.full((1, 128), scalars[1, 0], F32)
    weight = scalars[2, 0] * temperature / pairs

    def part(k, segment=0):
        return pl.ds(segment * rows + k * piece, piece)

    def slot_of(side, n, way, k, core=0):
        if n == 3:
            return far.at[side, part(k, core)]
        return ring.at[side, n, part(k, 2 * way + core)]

    def hop(side, n, way, k, src=None, peer=None):
        if src is None:
            src = own[side].at[part(k)] if n == 0 else slot_of(side, n - 1, way, k)
        if peer is None:
            peer = near_peer[side] if way == 0 else round_peer[side]
        return remote(
            src, slot_of(side, n, way, k), ring_sent.at[side, n, way, k], ring_landed.at[side, n, way, k], peer
        )

    def share(side, n, way, k):
        return remote(
            slot_of(side, n, way, k),
            slot_of(side, n, way, k, 1),
            core_sent.at[side, n, way, k],
            core_landed.at[side, n, way, k],
            core_peer,
        )

    def share_pair(side, n, way, h):
        src = ring.at[side, n, pl.ds(2 * way * rows + 2 * h * piece, 2 * piece)]
        dst = ring.at[side, n, pl.ds((2 * way + 1) * rows + 2 * h * piece, 2 * piece)]
        return remote(src, dst, core_sent.at[side, n, way, h], core_landed.at[side, n, way, h], core_peer)

    def cross(side, k):
        return remote(
            own[side].at[part(k)],
            crossed.at[side, part(k)],
            cross_sent.at[side, k],
            cross_landed.at[side, k],
            over[side],
        )

    def own_to_chip(side):
        src = (image_ref, text_ref)[side]
        return remote(src, col.at[side, pl.ds(rows, rows)], own_sent.at[side, 0], own_landed.at[side, 0], chip_peer)

    def own_to_core(side):
        return remote(
            own[side], trav.at[side, pl.ds(rows, rows)], own_sent.at[side, 1], own_landed.at[side, 1], core_peer
        )

    def chip_sum(side, k):
        return remote(
            slim_out.at[side, part(k)],
            slim_in.at[side, part(k)],
            sum_sent.at[side, k],
            sum_landed.at[side, k],
            chip_peer,
        )

    def result(side, k):
        out = (image_out, text_out)[side]
        return pltpu.make_async_copy(grad.at[side, part(k)], out.at[part(k)], out_done.at[side, k])

    def score(side, home, shards, first=False):
        logits = (
            lax.dot_general(
                col[side, home], shards[...], (((1,), (1,)), ((), ())), preferred_element_type=F32
            )
            * temperature[:, :1]
            + shift[:, :1]
        )
        values = jax.nn.sigmoid(logits)
        if first:
            i = lax.broadcasted_iota(jnp.int32, values.shape, 0)
            j = lax.broadcasted_iota(jnp.int32, values.shape, 1)
            values = values - jnp.where((i == j) & (i < rows), 1.0, 0.0)
        coefficient = values.astype(BF16)
        product = jnp.dot(coefficient, shards[...], preferred_element_type=F32)
        if first:
            acc[side, home] = product
        else:
            acc[side, home] += product

    own_rows, chip_rows, all_rows = pl.ds(0, rows), pl.ds(rows, rows), pl.ds(0, 2 * rows)

    def score_hop(side, n, k):
        if k == 1:
            score(side, all_rows, ring.at[side, n])

    def near_start(side, k):
        @pl.when(z != first[side])
        def _():
            hop(side, 0, 0, k).start()

    def cross_start(side, k):
        @pl.when(z != last[side])
        def _():
            cross(side, k).start()

        @pl.when(z == last[side])
        def _():
            hop(side, 0, 1, k, peer=end_peer[1 - side]).start()

    def relay(side, k):
        @pl.when(z != last[side])
        def _():
            cross(side, k).wait_recv()
            hop(side, 0, 1, k, src=crossed.at[side, part(k)]).start()

        @pl.when(z == first[side])
        def _():
            hop(side, 0, 0, k, src=crossed.at[side, part(k)], peer=end_peer[side]).start()

    def take(side, n, way, k):
        hop(side, n, way, k).wait_recv()
        if k % 2:
            share_pair(side, n, way, k // 2).start()
        if n < 2:
            hop(side, n + 1, way, k).start()
        else:

            if (k < HALF) == (way == 1):
                hop(side, 3, way, k).start()


    def on_far(method, make, side, k):
        getattr(make(side, 3, 1 - k // HALF, k), method)()

    def take_far(side, k):
        on_far("wait_recv", hop, side, k)
        on_far("start", share, side, k)

    def shared(side, n):
        for k in range(PIECES):
            if n == 3:
                on_far("wait_recv", share, side, k)
            else:
                for way in (0, 1):
                    if k % 2:
                        share_pair(side, n, way, k // 2).wait_recv()

    def swap(side):
        score(side, chip_rows, far.at[side])
        for k in range(PIECES):
            slim_out[side, part(k)] = acc[side, part(k, 1)].astype(BF16)
            chip_sum(side, k).start()

    def close(side):
        for k in range(PIECES):
            chip_sum(side, k).wait_recv()
            grad[side, part(k)] = (acc[side, part(k)] + slim_in[side, part(k)].astype(F32))
            result(side, k).start()

    for k in range(PIECES):
        cross_start(0, k)
        cross_start(1, k)
        near_start(0, k)
        near_start(1, k)

    for side in (0, 1):
        own_to_chip(side).start()
        own_to_core(side).start()

    for k in range(PIECES):
        relay(0, k)
        relay(1, k)
        take(0, 0, 0, k)
        take(1, 0, 0, k)

    for side in (0, 1):
        own_to_core(side).wait_recv()
        own_to_chip(side).wait_recv()

    for k in range(PIECES):
        take(0, 1, 0, k)
        take(1, 1, 0, k)
        take(0, 0, 1, k)
        take(1, 0, 1, k)
        if k % 2 == 0:
            score(k // 2, all_rows, trav.at[k // 2], first=True)


    shared(0, 0)

    for k in range(PIECES):
        take(0, 2, 0, k)
        take(0, 1, 1, k)
        score_hop(0, 0, k)

    shared(1, 0)

    for k in range(HALF):
        take(0, 2, 1, k)
        score_hop(1, 0, k)

    shared(0, 1)

    for k in range(PIECES):
        take(1, 1, 1, k)
        take(1, 2, 0, k)
        if k >= HALF:
            take(0, 2, 1, k)
        score_hop(0, 1, k)

    shared(0, 2)
    shared(1, 1)

    for k in (*range(HALF, PIECES), *range(HALF)):
        take_far(0, k)
        score_hop(0, 2, k)

    shared(0, 3)

    for k in range(PIECES):
        take(1, 2, 1, k)

        if k == 1:
            swap(0)
        if k == 2:
            score(0, own_rows, far.at[0])

        score_hop(1, 1, k)

    shared(1, 2)

    for k in (*range(HALF, PIECES), *range(HALF)):
        take_far(1, k)
        score_hop(1, 2, k)

    shared(1, 3)
    swap(1)
    score(1, own_rows, far.at[1])
    close(0)

    for side in (0, 1):
        own_to_chip(side).wait_send()
        own_to_core(side).wait_send()

        for k in range(PIECES):
            @pl.when(z != last[side])
            def _():
                cross(side, k).wait_send()

            for n in range(3):
                for way in (0, 1):
                    hop(side, n, way, k).wait_send()
                    if k % 2:
                        share_pair(side, n, way, k // 2).wait_send()
            on_far("wait_send", hop, side, k)
            on_far("wait_send", share, side, k)

    close(1)
    for side in (0, 1):
        for k in range(PIECES):
            chip_sum(side, k).wait_send()
            result(side, k).wait()


def local(
    picture_vectors,
    caption_vectors,
    natural_sharpness_exponent,
    trained_shift_term,
    objective_factor,
):
    rows, width = picture_vectors.shape
    groups = lax.axis_size("blk")
    columns = lax.axis_size("fsdp")
    pairs = rows * groups * columns
    hbm = pl.BlockSpec(memory_space=pltpu.HBM)
    out = jax.ShapeDtypeStruct((rows, width), F32)
    sems = pltpu.SemaphoreType.DMA
    grads = pl.pallas_call(
        functools.partial(kernel, columns, pairs),
        out_shape=(out, out),
        in_specs=[hbm] * 5,
        out_specs=(hbm, hbm),
        scratch_shapes=[
            pltpu.VMEM((2, 2 * rows, width), BF16),
            pltpu.VMEM((2, 2 * rows, width), BF16),
            pltpu.VMEM((2, rows, width), BF16),
            pltpu.VMEM((2, 3, 4 * rows, width), BF16),
            pltpu.VMEM((2, 2 * rows, width), BF16),
            pltpu.VMEM((2, 2 * rows, width), F32),
            pltpu.VMEM((2, rows, width), BF16),
            pltpu.VMEM((2, rows, width), BF16),
            sems((2, 4, 2, PIECES)),
            sems((2, 4, 2, PIECES)),
            sems((2, 4, 2, PIECES)),
            sems((2, 4, 2, PIECES)),
            sems((2, PIECES)),
            sems((2, PIECES)),
            sems((2, 2)),
            sems((2, 2)),
            sems((2, PIECES)),
            sems((2, PIECES)),
            sems((7,)),
            sems((2, PIECES)),
            pltpu.VMEM((2, rows, width), F32),
            pltpu.SMEM((3, 1), F32),
        ],
        compiler_params=pltpu.CompilerParams(
            collective_id=0, has_side_effects=True, vmem_limit_bytes=56 * 1024 * 1024
        ),
        cost_estimate=pl.CostEstimate(
            flops=2 * 4 * SPAN * groups * rows * rows * width,
            bytes_accessed=12 * rows * width,
            transcendentals=2 * SPAN * groups * rows * rows,
        ),
    )(
        natural_sharpness_exponent,
        trained_shift_term,
        objective_factor,
        picture_vectors,
        caption_vectors,
    )
    scale = objective_factor[0] * jnp.exp(natural_sharpness_exponent[0]) / pairs
    return scale * grads[0], scale * grads[1]


def solution(mesh):
    return jax.shard_map(
        local,
        mesh=mesh,
        in_specs=(P(("blk", "fsdp"), None), P(("blk", "fsdp"), None), P(), P(), P()),
        out_specs=(P(("blk", "fsdp"), None), P(("blk", "fsdp"), None)),
        check_vma=False,
    )
```

```python
import functools

import jax
import jax.numpy as jnp
from jax import lax
from jax.experimental import pallas as pl
from jax.experimental.pallas import tpu as pltpu
from jax.sharding import PartitionSpec as P

SPAN = 8
LINE = 8
PIECES = 4
HALF = 0

MESH = pl.DeviceIdType.MESH
F32 = jnp.float32
BF16 = jnp.bfloat16


def remote(src, dst, sent, landed, device):
    return pltpu.make_async_remote_copy(
        src_ref=src,
        dst_ref=dst,
        send_sem=sent,
        recv_sem=landed,
        device_id=device,
        device_id_type=MESH,
    )


def kernel(
    columns,
    pairs,
    exponent_ref,
    shift_ref,
    factor_ref,
    image_ref,
    text_ref,
    image_out,
    text_out,
    col,
    trav,
    crossed,
    ring,
    far,
    acc,
    slim_out,
    slim_in,
    ring_sent,
    ring_landed,
    core_sent,
    core_landed,
    cross_sent,
    cross_landed,
    own_sent,
    own_landed,
    sum_sent,
    sum_landed,
    local_done,
    out_done,
    grad,
    scalars,
):
    rows, width = image_ref.shape
    piece = rows // PIECES
    lines = columns // LINE
    b = lax.axis_index("blk")
    c = lax.axis_index("fsdp")
    z = lax.rem(c, LINE)

    def column_at(offset):
        other = lax.rem(c + offset + columns, columns)
        change = lax.rem(other // LINE - c // LINE + lines, lines)
        return (lax.rem(b + 2 * lax.rem(change, 2), 4), other)

    core_peer = (b + 1 - 2 * lax.rem(b, 2), c)
    chip_peer = (lax.rem(b + 2, 4), c)
    back, ahead = column_at(-1), column_at(1)
    over = (column_at(-LINE), column_at(LINE))
    end_peer = (column_at(LINE - 1), column_at(1 - LINE))
    first, last = (0, LINE - 1), (LINE - 1, 0)
    own = (text_ref, image_ref)
    near_peer, round_peer = (back, ahead), (ahead, back)

    local = [
        pltpu.make_async_copy(src, dst, local_done.at[i])
        for i, (src, dst) in enumerate(
            (
                (image_ref, col.at[0, pl.ds(0, rows)]),
                (text_ref, col.at[1, pl.ds(0, rows)]),
                (text_ref, trav.at[0, pl.ds(0, rows)]),
                (image_ref, trav.at[1, pl.ds(0, rows)]),
                (exponent_ref, scalars.at[0]),
                (shift_ref, scalars.at[1]),
                (factor_ref, scalars.at[2]),
            )
        )
    ]
    for copy in local:
        copy.start()

    barrier = pltpu.get_barrier_semaphore()
    for device in (back, ahead, *over, core_peer, chip_peer):
        pl.semaphore_signal(barrier, inc=1, device_id=device, device_id_type=MESH)
    for side in (0, 1):

        @pl.when(z == first[side])
        def _():
            pl.semaphore_signal(barrier, inc=1, device_id=end_peer[side], device_id_type=MESH)
            pl.semaphore_wait(barrier, 7)

    @pl.when(lax.rem(z, LINE - 1) != 0)
    def _():
        pl.semaphore_wait(barrier, 6)

    for copy in local:
        copy.wait()
    temperature = jnp.exp(jnp.full((1, 128), scalars[0, 0], F32))
    shift = jnp.full((1, 128), scalars[1, 0], F32)
    weight = scalars[2, 0] * temperature / pairs

    def part(k, segment=0):
        return pl.ds(segment * rows + k * piece, piece)

    def slot_of(side, n, way, k, core=0):
        if n == 3:
            return far.at[side, part(k, core)]
        return ring.at[side, n, part(k, 2 * way + core)]

    def hop(side, n, way, k, src=None, peer=None):
        if src is None:
            src = own[side].at[part(k)] if n == 0 else slot_of(side, n - 1, way, k)
        if peer is None:
            peer = near_peer[side] if way == 0 else round_peer[side]
        return remote(
            src, slot_of(side, n, way, k), ring_sent.at[side, n, way, k], ring_landed.at[side, n, way, k], peer
        )

    def share(side, n, way, k):
        return remote(
            slot_of(side, n, way, k),
            slot_of(side, n, way, k, 1),
            core_sent.at[side, n, way, k],
            core_landed.at[side, n, way, k],
            core_peer,
        )

    def share_pair(side, n, way, h):
        src = ring.at[side, n, pl.ds(2 * way * rows + 2 * h * piece, 2 * piece)]
        dst = ring.at[side, n, pl.ds((2 * way + 1) * rows + 2 * h * piece, 2 * piece)]
        return remote(src, dst, core_sent.at[side, n, way, h], core_landed.at[side, n, way, h], core_peer)

    def cross(side, k):
        return remote(
            own[side].at[part(k)],
            crossed.at[side, part(k)],
            cross_sent.at[side, k],
            cross_landed.at[side, k],
            over[side],
        )

    def own_to_chip(side):
        src = (image_ref, text_ref)[side]
        return remote(src, col.at[side, pl.ds(rows, rows)], own_sent.at[side, 0], own_landed.at[side, 0], chip_peer)

    def own_to_core(side):
        return remote(
            own[side], trav.at[side, pl.ds(rows, rows)], own_sent.at[side, 1], own_landed.at[side, 1], core_peer
        )

    def chip_sum(side, k):
        return remote(
            slim_out.at[side, part(k)],
            slim_in.at[side, part(k)],
            sum_sent.at[side, k],
            sum_landed.at[side, k],
            chip_peer,
        )

    def result(side, k):
        out = (image_out, text_out)[side]
        return pltpu.make_async_copy(grad.at[side, part(k)], out.at[part(k)], out_done.at[side, k])

    def score(side, home, shards, first=False):
        logits = (
            lax.dot_general(
                col[side, home], shards[...], (((1,), (1,)), ((), ())), preferred_element_type=F32
            )
            * temperature[:, :1]
            + shift[:, :1]
        )
        values = jax.nn.sigmoid(logits)
        if first:
            i = lax.broadcasted_iota(jnp.int32, values.shape, 0)
            j = lax.broadcasted_iota(jnp.int32, values.shape, 1)
            values = values - jnp.where((i == j) & (i < rows), 1.0, 0.0)
        coefficient = values.astype(BF16)
        product = jnp.dot(coefficient, shards[...], preferred_element_type=F32)
        if first:
            acc[side, home] = product
        else:
            acc[side, home] += product

    own_rows, chip_rows, all_rows = pl.ds(0, rows), pl.ds(rows, rows), pl.ds(0, 2 * rows)

    def score_hop(side, n, k):
        if k == 1:
            score(side, all_rows, ring.at[side, n])

    def near_start(side, k):
        @pl.when(z != first[side])
        def _():
            hop(side, 0, 0, k).start()

    def cross_start(side, k):
        @pl.when(z != last[side])
        def _():
            cross(side, k).start()

        @pl.when(z == last[side])
        def _():
            hop(side, 0, 1, k, peer=end_peer[1 - side]).start()

    def relay(side, k):
        @pl.when(z != last[side])
        def _():
            cross(side, k).wait_recv()
            hop(side, 0, 1, k, src=crossed.at[side, part(k)]).start()

        @pl.when(z == first[side])
        def _():
            hop(side, 0, 0, k, src=crossed.at[side, part(k)], peer=end_peer[side]).start()

    def take(side, n, way, k):
        hop(side, n, way, k).wait_recv()
        if k % 2:
            share_pair(side, n, way, k // 2).start()
        if n < 2:
            hop(side, n + 1, way, k).start()
        else:

            if (k < HALF) == (way == 1):
                hop(side, 3, way, k).start()


    def on_far(method, make, side, k):
        getattr(make(side, 3, 1 if k < HALF else 0, k), method)()

    def take_far(side, k):
        on_far("wait_recv", hop, side, k)
        on_far("start", share, side, k)

    def shared(side, n):
        for k in range(PIECES):
            if n == 3:
                on_far("wait_recv", share, side, k)
            else:
                for way in (0, 1):
                    if k % 2:
                        share_pair(side, n, way, k // 2).wait_recv()

    def swap(side):
        score(side, chip_rows, far.at[side])
        for k in range(PIECES):
            slim_out[side, part(k)] = acc[side, part(k, 1)].astype(BF16)
            chip_sum(side, k).start()

    def close(side):
        for k in range(PIECES):
            chip_sum(side, k).wait_recv()
            grad[side, part(k)] = (acc[side, part(k)] + slim_in[side, part(k)].astype(F32))
            result(side, k).start()

    for k in range(PIECES):
        cross_start(0, k)
        cross_start(1, k)
        near_start(0, k)
        near_start(1, k)

    for side in (0, 1):
        own_to_chip(side).start()
        own_to_core(side).start()

    for k in range(PIECES):
        relay(0, k)
        relay(1, k)
        take(0, 0, 0, k)
        take(1, 0, 0, k)

    for side in (0, 1):
        own_to_core(side).wait_recv()
        own_to_chip(side).wait_recv()

    for k in range(PIECES):
        take(0, 1, 0, k)
        take(1, 1, 0, k)
        take(0, 0, 1, k)
        take(1, 0, 1, k)
        if k % 2 == 0:
            score(k // 2, all_rows, trav.at[k // 2], first=True)


    shared(0, 0)

    for k in range(PIECES):
        take(0, 2, 0, k)
        take(0, 1, 1, k)
        score_hop(0, 0, k)

    shared(1, 0)

    for k in range(HALF):
        take(0, 2, 1, k)

    score_hop(1, 0, 1)

    shared(0, 1)

    for k in range(PIECES):
        take(1, 1, 1, k)
        take(1, 2, 0, k)
        if k >= HALF:
            take(0, 2, 1, k)
        score_hop(0, 1, k)

    shared(0, 2)
    shared(1, 1)

    for k in (*range(HALF, PIECES), *range(HALF)):
        take_far(0, k)
        score_hop(0, 2, k)

    shared(0, 3)

    for k in range(PIECES):
        take(1, 2, 1, k)

        if k == 1:
            swap(0)
        if k == 2:
            score(0, own_rows, far.at[0])

        score_hop(1, 1, k)

    shared(1, 2)

    for k in (*range(HALF, PIECES), *range(HALF)):
        take_far(1, k)
        score_hop(1, 2, k)

    shared(1, 3)
    swap(1)
    score(1, own_rows, far.at[1])
    close(0)

    for side in (0, 1):
        own_to_chip(side).wait_send()
        own_to_core(side).wait_send()

        for k in range(PIECES):
            @pl.when(z != last[side])
            def _():
                cross(side, k).wait_send()

            for n in range(3):
                for way in (0, 1):
                    hop(side, n, way, k).wait_send()
                    if k % 2:
                        share_pair(side, n, way, k // 2).wait_send()
            on_far("wait_send", hop, side, k)
            on_far("wait_send", share, side, k)

    close(1)
    for side in (0, 1):
        for k in range(PIECES):
            chip_sum(side, k).wait_send()
            result(side, k).wait()


def local(
    picture_vectors,
    caption_vectors,
    natural_sharpness_exponent,
    trained_shift_term,
    objective_factor,
):
    rows, width = picture_vectors.shape
    groups = lax.axis_size("blk")
    columns = lax.axis_size("fsdp")
    pairs = rows * groups * columns
    hbm = pl.BlockSpec(memory_space=pltpu.HBM)
    out = jax.ShapeDtypeStruct((rows, width), F32)
    sems = pltpu.SemaphoreType.DMA
    grads = pl.pallas_call(
        functools.partial(kernel, columns, pairs),
        out_shape=(out, out),
        in_specs=[hbm] * 5,
        out_specs=(hbm, hbm),
        scratch_shapes=[
            pltpu.VMEM((2, 2 * rows, width), BF16),
            pltpu.VMEM((2, 2 * rows, width), BF16),
            pltpu.VMEM((2, rows, width), BF16),
            pltpu.VMEM((2, 3, 4 * rows, width), BF16),
            pltpu.VMEM((2, 2 * rows, width), BF16),
            pltpu.VMEM((2, 2 * rows, width), F32),
            pltpu.VMEM((2, rows, width), BF16),
            pltpu.VMEM((2, rows, width), BF16),
            sems((2, 4, 2, PIECES)),
            sems((2, 4, 2, PIECES)),
            sems((2, 4, 2, PIECES)),
            sems((2, 4, 2, PIECES)),
            sems((2, PIECES)),
            sems((2, PIECES)),
            sems((2, 2)),
            sems((2, 2)),
            sems((2, PIECES)),
            sems((2, PIECES)),
            sems((7,)),
            sems((2, PIECES)),
            pltpu.VMEM((2, rows, width), F32),
            pltpu.SMEM((3, 1), F32),
        ],
        compiler_params=pltpu.CompilerParams(
            collective_id=0, has_side_effects=True, vmem_limit_bytes=56 * 1024 * 1024
        ),
        cost_estimate=pl.CostEstimate(
            flops=2 * 4 * SPAN * groups * rows * rows * width,
            bytes_accessed=12 * rows * width,
            transcendentals=2 * SPAN * groups * rows * rows,
        ),
    )(
        natural_sharpness_exponent,
        trained_shift_term,
        objective_factor,
        picture_vectors,
        caption_vectors,
    )
    scale = objective_factor[0] * jnp.exp(natural_sharpness_exponent[0]) / pairs
    return scale * grads[0], scale * grads[1]


def solution(mesh):
    return jax.shard_map(
        local,
        mesh=mesh,
        in_specs=(P(("blk", "fsdp"), None), P(("blk", "fsdp"), None), P(), P(), P()),
        out_specs=(P(("blk", "fsdp"), None), P(("blk", "fsdp"), None)),
        check_vma=False,
    )
```

```python
import functools

import jax
import jax.numpy as jnp
from jax import lax
from jax.experimental import pallas as pl
from jax.experimental.pallas import tpu as pltpu
from jax.sharding import PartitionSpec as P

SPAN = 8
LINE = 8
PIECES = 4
HALF = 0

MESH = pl.DeviceIdType.MESH
F32 = jnp.float32
BF16 = jnp.bfloat16


def remote(src, dst, sent, landed, device):
    return pltpu.make_async_remote_copy(
        src_ref=src,
        dst_ref=dst,
        send_sem=sent,
        recv_sem=landed,
        device_id=device,
        device_id_type=MESH,
    )


def kernel(
    columns,
    pairs,
    exponent_ref,
    shift_ref,
    factor_ref,
    image_ref,
    text_ref,
    image_out,
    text_out,
    col,
    trav,
    crossed,
    ring,
    far,
    acc,
    slim_out,
    slim_in,
    ring_sent,
    ring_landed,
    core_sent,
    core_landed,
    cross_sent,
    cross_landed,
    own_sent,
    own_landed,
    sum_sent,
    sum_landed,
    local_done,
    out_done,
    grad,
    scalars,
):
    rows, width = image_ref.shape
    piece = rows // PIECES
    lines = columns // LINE
    b = lax.axis_index("blk")
    c = lax.axis_index("fsdp")
    z = lax.rem(c, LINE)

    def column_at(offset):
        other = lax.rem(c + offset + columns, columns)
        change = lax.rem(other // LINE - c // LINE + lines, lines)
        return (lax.rem(b + 2 * lax.rem(change, 2), 4), other)

    core_peer = (b + 1 - 2 * lax.rem(b, 2), c)
    chip_peer = (lax.rem(b + 2, 4), c)
    back, ahead = column_at(-1), column_at(1)
    over = (column_at(-LINE), column_at(LINE))
    end_peer = (column_at(LINE - 1), column_at(1 - LINE))
    first, last = (0, LINE - 1), (LINE - 1, 0)
    own = (text_ref, image_ref)
    near_peer, round_peer = (back, ahead), (ahead, back)

    local = [
        pltpu.make_async_copy(src, dst, local_done.at[i])
        for i, (src, dst) in enumerate(
            (
                (image_ref, col.at[0, pl.ds(0, rows)]),
                (text_ref, col.at[1, pl.ds(0, rows)]),
                (text_ref, trav.at[0, pl.ds(0, rows)]),
                (image_ref, trav.at[1, pl.ds(0, rows)]),
                (exponent_ref, scalars.at[0]),
                (shift_ref, scalars.at[1]),
                (factor_ref, scalars.at[2]),
            )
        )
    ]
    for copy in local:
        copy.start()

    barrier = pltpu.get_barrier_semaphore()
    for device in (back, ahead, *over, core_peer, chip_peer):
        pl.semaphore_signal(barrier, inc=1, device_id=device, device_id_type=MESH)
    for side in (0, 1):

        @pl.when(z == first[side])
        def _():
            pl.semaphore_signal(barrier, inc=1, device_id=end_peer[side], device_id_type=MESH)
            pl.semaphore_wait(barrier, 7)

    @pl.when(lax.rem(z, LINE - 1) != 0)
    def _():
        pl.semaphore_wait(barrier, 6)

    for copy in local:
        copy.wait()
    temperature = jnp.exp(jnp.full((1, 128), scalars[0, 0], F32))
    shift = jnp.full((1, 128), scalars[1, 0], F32)
    weight = scalars[2, 0] * temperature / pairs

    def part(k, segment=0):
        return pl.ds(segment * rows + k * piece, piece)

    def slot_of(side, n, way, k, core=0):
        if n == 3:
            return far.at[side, part(k, core)]
        return ring.at[side, n, part(k, 2 * way + core)]

    def hop(side, n, way, k, src=None, peer=None):
        if src is None:
            src = own[side].at[part(k)] if n == 0 else slot_of(side, n - 1, way, k)
        if peer is None:
            peer = near_peer[side] if way == 0 else round_peer[side]
        return remote(
            src, slot_of(side, n, way, k), ring_sent.at[side, n, way, k], ring_landed.at[side, n, way, k], peer
        )

    def share(side, n, way, k):
        return remote(
            slot_of(side, n, way, k),
            slot_of(side, n, way, k, 1),
            core_sent.at[side, n, way, k],
            core_landed.at[side, n, way, k],
            core_peer,
        )

    def share_pair(side, n, way, h):
        src = ring.at[side, n, pl.ds(2 * way * rows + 2 * h * piece, 2 * piece)]
        dst = ring.at[side, n, pl.ds((2 * way + 1) * rows + 2 * h * piece, 2 * piece)]
        return remote(src, dst, core_sent.at[side, n, way, h], core_landed.at[side, n, way, h], core_peer)

    def cross(side, k):
        return remote(
            own[side].at[part(k)],
            crossed.at[side, part(k)],
            cross_sent.at[side, k],
            cross_landed.at[side, k],
            over[side],
        )

    def own_to_chip(side):
        src = (image_ref, text_ref)[side]
        return remote(src, col.at[side, pl.ds(rows, rows)], own_sent.at[side, 0], own_landed.at[side, 0], chip_peer)

    def own_to_core(side):
        return remote(
            own[side], trav.at[side, pl.ds(rows, rows)], own_sent.at[side, 1], own_landed.at[side, 1], core_peer
        )

    def chip_sum(side, k):
        return remote(
            slim_out.at[side, part(k)],
            slim_in.at[side, part(k)],
            sum_sent.at[side, k],
            sum_landed.at[side, k],
            chip_peer,
        )

    def result(side, k):
        out = (image_out, text_out)[side]
        return pltpu.make_async_copy(grad.at[side, part(k)], out.at[part(k)], out_done.at[side, k])

    def score(side, home, shards, first=False):
        logits = (
            lax.dot_general(
                col[side, home], shards[...], (((1,), (1,)), ((), ())), preferred_element_type=F32
            )
            * temperature[:, :1]
            + shift[:, :1]
        )
        values = jax.nn.sigmoid(logits)
        if first:
            i = lax.broadcasted_iota(jnp.int32, values.shape, 0)
            j = lax.broadcasted_iota(jnp.int32, values.shape, 1)
            values = values - jnp.where((i == j) & (i < rows), 1.0, 0.0)
        coefficient = values.astype(BF16)
        product = jnp.dot(coefficient, shards[...], preferred_element_type=F32)
        if first:
            acc[side, home] = product
        else:
            acc[side, home] += product

    own_rows, all_rows = pl.ds(0, rows), pl.ds(0, 2 * rows)

    def score_hop(side, n, k):
        if k == 1:
            score(side, all_rows, ring.at[side, n])

    def near_start(side, k):
        @pl.when(z != first[side])
        def _():
            hop(side, 0, 0, k).start()

    def cross_start(side, k):
        @pl.when(z != last[side])
        def _():
            cross(side, k).start()

        @pl.when(z == last[side])
        def _():
            hop(side, 0, 1, k, peer=end_peer[1 - side]).start()

    def relay(side, k):
        @pl.when(z != last[side])
        def _():
            cross(side, k).wait_recv()
            hop(side, 0, 1, k, src=crossed.at[side, part(k)]).start()

        @pl.when(z == first[side])
        def _():
            hop(side, 0, 0, k, src=crossed.at[side, part(k)], peer=end_peer[side]).start()

    def take(side, n, way, k):
        hop(side, n, way, k).wait_recv()
        if k % 2:
            share_pair(side, n, way, k // 2).start()
        if n < 2:
            hop(side, n + 1, way, k).start()
        else:

            if (k < HALF) == (way == 1):
                hop(side, 3, way, k).start()


    def on_far(method, make, side, k):
        getattr(make(side, 3, 1 if k < HALF else 0, k), method)()

    def take_far(side, k):
        on_far("wait_recv", hop, side, k)
        on_far("start", share, side, k)

    def shared(side, n):
        for k in range(PIECES):
            if n == 3:
                on_far("wait_recv", share, side, k)
            else:
                for way in (0, 1):
                    if k % 2:
                        share_pair(side, n, way, k // 2).wait_recv()

    def swap(side, *shards):
        for h in (0, 1):
            for some in shards:
                score(side, pl.ds(rows + h * rows // 2, rows // 2), some)
            for k in range(h * PIECES // 2, (h + 1) * PIECES // 2):
                slim_out[side, part(k)] = acc[side, part(k, 1)].astype(BF16)
                chip_sum(side, k).start()

    def close(side):
        for k in range(PIECES):
            chip_sum(side, k).wait_recv()
            grad[side, part(k)] = (acc[side, part(k)] + slim_in[side, part(k)].astype(F32))
            result(side, k).start()

    for k in range(PIECES):
        cross_start(0, k)
        cross_start(1, k)
        near_start(0, k)
        near_start(1, k)

    for side in (0, 1):
        own_to_chip(side).start()
        own_to_core(side).start()

    for k in range(PIECES):
        relay(0, k)
        relay(1, k)
        take(0, 0, 0, k)
        take(1, 0, 0, k)

    for side in (0, 1):
        own_to_core(side).wait_recv()
        own_to_chip(side).wait_recv()

    for k in range(PIECES):
        take(0, 1, 0, k)
        take(1, 1, 0, k)
        take(0, 0, 1, k)
        take(1, 0, 1, k)
        if k % 2 == 0:
            score(k // 2, all_rows, trav.at[k // 2], first=True)


    shared(0, 0)

    for k in range(PIECES):
        take(0, 2, 0, k)
        take(0, 1, 1, k)
        score_hop(0, 0, k)

    shared(1, 0)

    for k in range(HALF):
        take(0, 2, 1, k)

    score_hop(1, 0, 1)

    shared(0, 1)

    for k in range(PIECES):
        take(1, 1, 1, k)
        take(1, 2, 0, k)
        if k >= HALF:
            take(0, 2, 1, k)
        score_hop(0, 1, k)

    shared(0, 2)
    shared(1, 1)

    for k in (*range(HALF, PIECES), *range(HALF)):
        take_far(0, k)
        score_hop(0, 2, k)

    shared(0, 3)

    swap(0, far.at[0])
    score(0, own_rows, far.at[0])

    for k in range(PIECES):
        take(1, 2, 1, k)
        take_far(1, k)
        score_hop(1, 1, k)

    shared(1, 2)
    shared(1, 3)
    swap(1, ring.at[1, 2], far.at[1])
    score(1, own_rows, ring.at[1, 2])
    score(1, own_rows, far.at[1])
    close(0)

    for side in (0, 1):
        own_to_chip(side).wait_send()
        own_to_core(side).wait_send()

        for k in range(PIECES):
            @pl.when(z != last[side])
            def _():
                cross(side, k).wait_send()

            for n in range(3):
                for way in (0, 1):
                    hop(side, n, way, k).wait_send()
                    if k % 2:
                        share_pair(side, n, way, k // 2).wait_send()
            on_far("wait_send", hop, side, k)
            on_far("wait_send", share, side, k)

    close(1)
    for side in (0, 1):
        for k in range(PIECES):
            chip_sum(side, k).wait_send()
            result(side, k).wait()


def local(
    picture_vectors,
    caption_vectors,
    natural_sharpness_exponent,
    trained_shift_term,
    objective_factor,
):
    rows, width = picture_vectors.shape
    groups = lax.axis_size("blk")
    columns = lax.axis_size("fsdp")
    pairs = rows * groups * columns
    hbm = pl.BlockSpec(memory_space=pltpu.HBM)
    out = jax.ShapeDtypeStruct((rows, width), F32)
    sems = pltpu.SemaphoreType.DMA
    grads = pl.pallas_call(
        functools.partial(kernel, columns, pairs),
        out_shape=(out, out),
        in_specs=[hbm] * 5,
        out_specs=(hbm, hbm),
        scratch_shapes=[
            pltpu.VMEM((2, 2 * rows, width), BF16),
            pltpu.VMEM((2, 2 * rows, width), BF16),
            pltpu.VMEM((2, rows, width), BF16),
            pltpu.VMEM((2, 3, 4 * rows, width), BF16),
            pltpu.VMEM((2, 2 * rows, width), BF16),
            pltpu.VMEM((2, 2 * rows, width), F32),
            pltpu.VMEM((2, rows, width), BF16),
            pltpu.VMEM((2, rows, width), BF16),
            sems((2, 4, 2, PIECES)),
            sems((2, 4, 2, PIECES)),
            sems((2, 4, 2, PIECES)),
            sems((2, 4, 2, PIECES)),
            sems((2, PIECES)),
            sems((2, PIECES)),
            sems((2, 2)),
            sems((2, 2)),
            sems((2, PIECES)),
            sems((2, PIECES)),
            sems((7,)),
            sems((2, PIECES)),
            pltpu.VMEM((2, rows, width), F32),
            pltpu.SMEM((3, 1), F32),
        ],
        compiler_params=pltpu.CompilerParams(
            collective_id=0, has_side_effects=True, vmem_limit_bytes=56 * 1024 * 1024
        ),
        cost_estimate=pl.CostEstimate(
            flops=2 * 4 * SPAN * groups * rows * rows * width,
            bytes_accessed=12 * rows * width,
            transcendentals=2 * SPAN * groups * rows * rows,
        ),
    )(
        natural_sharpness_exponent,
        trained_shift_term,
        objective_factor,
        picture_vectors,
        caption_vectors,
    )
    scale = objective_factor[0] * jnp.exp(natural_sharpness_exponent[0]) / pairs
    return scale * grads[0], scale * grads[1]


def solution(mesh):
    return jax.shard_map(
        local,
        mesh=mesh,
        in_specs=(P(("blk", "fsdp"), None), P(("blk", "fsdp"), None), P(), P(), P()),
        out_specs=(P(("blk", "fsdp"), None), P(("blk", "fsdp"), None)),
        check_vma=False,
    )
```
